32 devices in a mesh: seq: 4 (over z), wt: 8 (over y, x, core).
Axes of the slice: x: 2, y: 2, z: 4, core: 2. Of those that a mesh axis runs over, the one named last changes fastest.
Arguments:
- tokens_in: bfloat16 [896, 4608], P('seq', 'wt'), may hold values from -6 to 6
- norm_gain: float32 [4608], P('wt'), may hold values from 0.25 to 1.75
- positions: int32 [896], P('seq'), may hold values from 0 to 671, as said below
- blocks: bfloat16 [8, 16, 128, 128], P('wt'), may hold values from -0.125 to 0.125
- slot_code: int32 [8, 16], P('wt'), may hold values from -1 to 575, as said below
- out_grad: bfloat16 [896, 1024], P('seq', 'wt'), may hold values from -6 to 6
Outputs:
- attn_out: bfloat16 [896, 1024], P('seq', 'wt')
- tokens_grad: bfloat16 [896, 4608], P('seq', 'wt')
- gain_grad: float32 [4608], P('wt')
- block_grads: bfloat16 [8, 16, 128, 128], P('wt')
The draws below stay inside these ranges and needn't reach their ends.
Inputs may be any that keep to these rules, and one draw needn't show every extreme that they name: Positions count the tokens of each document from 0: positions[0] = 0 and every later entry is either 0 (a new document starts) or the entry before plus one. The longest document has exactly 672 tokens. slot_code[o, s] is -1 for an empty slot, else u * 2 * 36 + p with head u and 0 <= p < 72; no value other than -1 appears twice. One owner holds at most 2 blocks for one head; in every draw some owner holds 2 blocks for every head and some head has 2 blocks at every owner.
All inputs are finite; a program needn't handle non-finite values.
Results may differ from the reference program's by a relative error of at most 0.023.
Values may be sent and summed in bfloat16 or wider, within the bound.
A program may use at most 64 MiB of HBM per device.

```python
from functools import partial
import jax
import jax.numpy as jnp
from jax import lax

D = 4608
HD = 128
BLK = 128
CAP = 2
TOK_DEV = 224
HEADS = 8
RB = 36
SLOTS = 16
TOKENS = 896
WINDOW = 448
N_SEQ = 4
N_WT = 8


def order_of(sub_key, count):
    order = jax.random.permutation(sub_key, count)
    index = jnp.arange(count, dtype=jnp.int32)
    last_value = count - 1
    return jnp.where(index == 0, last_value, jnp.where(order == last_value, order[0], order))


def draw_slot_code(key, part):
    sub_keys = jax.random.split(key, 5)
    groups = N_WT
    pos_count = 2 * (D // BLK)
    counts = jax.random.randint(sub_keys[0], (groups, groups), 0, CAP + 1)
    full_owner = jax.random.randint(sub_keys[1], (), 0, groups)
    full_user = jax.random.randint(sub_keys[2], (), 0, groups)
    owner_ids = jnp.arange(groups, dtype=jnp.int32)[:, None]
    user_ids = jnp.arange(groups, dtype=jnp.int32)[None, :]
    forced = (owner_ids == full_owner) | (user_ids == full_user) | (owner_ids == 0) & (user_ids == groups - 1)
    counts = jnp.where(forced, CAP, counts)
    earlier = jnp.cumsum(counts, axis=0) - counts
    orders = jax.vmap(partial(order_of, count=pos_count))(jax.random.split(sub_keys[3], groups))
    within = jnp.arange(CAP, dtype=jnp.int32)[None, None, :]
    pick_index = jnp.minimum(earlier[:, :, None] + within, pos_count - 1)
    chosen = jnp.take_along_axis(jnp.broadcast_to(orders[None], (groups, groups, pos_count)), pick_index, axis=2)
    is_live = within < counts[:, :, None]
    codes = jnp.where(is_live, user_ids[:, :, None] * pos_count + chosen, -1).reshape(groups, groups * CAP)
    shuffle = jax.vmap(jax.random.permutation, in_axes=(0, None))(jax.random.split(sub_keys[4], groups), groups * CAP)
    return jnp.take_along_axis(codes, shuffle, axis=1).astype(jnp.int32)


def draw_positions(key, part):
    sub_keys = jax.random.split(key, 2)
    long_doc = 3 * TOKENS // 4
    long_start = jax.random.randint(sub_keys[0], (), 0, TOKENS - long_doc + 1)
    extra_cut = jax.random.randint(sub_keys[1], (), 1, TOKENS)
    extra_ok = (extra_cut <= long_start) | (extra_cut >= long_start + long_doc)
    token_index = jnp.arange(TOKENS, dtype=jnp.int32)
    is_start = (token_index == 0) | (token_index == long_start) | (token_index == long_start + long_doc) | (token_index == extra_cut) & extra_ok
    starts = jnp.where(is_start, token_index, 0)
    return (token_index - lax.cummax(starts, axis=0)).astype(jnp.int32)


def block_scale(key, shape, pieces, low, largest):
    loudness = 1.0
    for position, shards_of in pieces:
        heights = jax.random.uniform(jax.random.fold_in(jax.random.fold_in(key, 6), position), (shards_of,), jnp.float32, low / len(pieces), largest / len(pieces))
        loudness = loudness * jnp.repeat(jnp.exp(heights), shape[position] // shards_of).reshape((-1,) + (1,) * (len(shape) - 1 - position))
    return loudness


def noise(rng, shape, spread, reach, cuts=(), kind=jnp.bfloat16):
    array = jax.random.normal(rng, shape, jnp.float32) * spread
    if len(cuts) > 0:
        array = block_scale(rng, shape, cuts, -0.22, 0.18) * array
    return jnp.clip(array, min=-reach, max=reach).astype(kind)


def setup_inputs(seed: int = 0) -> dict:
    seeds = jax.random.split(jax.random.key(seed), 7)
    tokens_in = noise(seeds[0], (TOKENS, D), 1.0, 6.0, ((0, 4), (1, 8)))
    norm_gain = jnp.clip(1.0 + 0.15 * jax.random.normal(seeds[1], (D,), jnp.float32), 0.25, 1.75)
    positions = draw_positions(jax.random.fold_in(seeds[6], 71), 0)
    blocks = noise(seeds[3], (N_WT, SLOTS, BLK, BLK), (D // 2) ** -0.5, 0.125, ((0, 8),))
    slot_code = draw_slot_code(jax.random.fold_in(seeds[6], 71), 0)
    out_grad = noise(seeds[5], (TOKENS, HEADS * HD), 1.0, 6.0, ((0, 4), (1, 8)))
    return {"tokens_in": tokens_in, "norm_gain": norm_gain, "positions": positions, "blocks": blocks, "slot_code": slot_code, "out_grad": out_grad}


query_scale = 144.0 ** (-0.5)
soft_cap = 50.0
norm_eps = 1e-06

def rounded(values):
    return lax.optimization_barrier(values.astype(jnp.bfloat16)).astype(jnp.float32)

def rope_tables(positions, head_width):
    half_width = head_width // 2
    frequency = 10000.0 ** (-2.0 * jnp.arange(half_width, dtype=jnp.float32) / head_width)
    angles = positions.astype(jnp.float32)[:, None] * frequency[None, :]
    return (jnp.cos(angles), jnp.sin(angles))

def rotate(vector, cos_table, sin_table):
    half_width = vector.shape[-1] // 2
    first_half = vector[..., :half_width]
    second_half = vector[..., half_width:]
    return jnp.concatenate([first_half * cos_table - second_half * sin_table, first_half * sin_table + second_half * cos_table], axis=-1)

def reference(tokens_in, norm_gain, positions, blocks, slot_code, out_grad):
    tokens_f32 = tokens_in.astype(jnp.float32)
    inv_rms = lax.rsqrt(lax.optimization_barrier(jnp.mean(tokens_f32 * tokens_f32, axis=1)) + norm_eps)
    scaled = tokens_f32 * inv_rms[:, None]
    normed = (scaled * norm_gain[None, :]).astype(jnp.bfloat16)
    normed_f32 = normed.astype(jnp.float32)
    slab_normed = normed_f32.reshape(N_SEQ, TOK_DEV, D)
    pos_total = HEADS * 2 * RB
    slot_codes = slot_code.reshape(-1)
    flat_blocks = blocks.reshape(-1, BLK, BLK)
    block_target = jnp.where(slot_codes < 0, pos_total, slot_codes).astype(jnp.int32)
    weight_table = jnp.zeros((pos_total + 1, BLK, BLK), jnp.bfloat16).at[block_target].set(flat_blocks)
    weight_table = weight_table[:pos_total].reshape(HEADS, 2, D, HD)
    cos_table, sin_table = rope_tables(positions, HD)
    token_index = jnp.arange(TOKENS, dtype=jnp.int32)
    doc_begin = token_index - positions
    distance = token_index[:, None] - token_index[None, :]
    visible = (distance >= 0) & (distance < WINDOW) & (token_index[None, :] >= doc_begin[:, None])
    out_heads = out_grad.reshape(TOKENS, HEADS, HD).transpose(1, 0, 2)

    def group(normed_grad, group_index):
        first_head = (2 * group_index).astype(jnp.int32)
        pair_weights = lax.dynamic_slice_in_dim(weight_table, first_head, 2, 0)
        w_query = pair_weights[:, 0]
        w_key = pair_weights[0, 1]
        w_value = pair_weights[1, 1]
        query_proj = jnp.einsum('td,hdf->htf', normed_f32, w_query.astype(jnp.float32))
        key_proj = jnp.dot(normed, w_key, preferred_element_type=jnp.float32)
        value_proj = jnp.dot(normed, w_value, preferred_element_type=jnp.float32)
        query_rot = (rotate(query_proj, cos_table, sin_table) * query_scale).astype(jnp.bfloat16).astype(jnp.float32)
        key_rot = rotate(key_proj, cos_table, sin_table).astype(jnp.bfloat16).astype(jnp.float32)
        value_low = value_proj.astype(jnp.bfloat16).astype(jnp.float32)
        scores = jnp.einsum('htf,sf->hts', query_rot, key_rot)
        capped = soft_cap * jnp.tanh(scores / soft_cap)
        exp_scores = jnp.where(visible[None], jnp.exp(capped), 0.0)
        row_total = lax.optimization_barrier(jnp.sum(exp_scores, axis=2))
        head_out = (jnp.einsum('hts,sf->htf', rounded(exp_scores), value_low) / row_total[:, :, None]).astype(jnp.bfloat16)
        out_slice = lax.dynamic_slice_in_dim(out_heads, first_head, 2, 0).astype(jnp.float32)
        row_delta = lax.optimization_barrier(jnp.sum(out_slice * head_out.astype(jnp.float32), axis=2))
        soft_probs = exp_scores / row_total[:, :, None]
        prob_grad = jnp.einsum('htf,sf->hts', out_slice, value_low)
        score_grad = soft_probs * (prob_grad - row_delta[:, :, None]) * (1.0 - (capped / soft_cap) ** 2)
        score_low = rounded(score_grad)
        probs_low = rounded(soft_probs)
        rot_grad = jnp.einsum('hts,sf->htf', score_low, key_rot)
        query_grad = (rotate(rot_grad, cos_table, -sin_table) * query_scale).astype(jnp.bfloat16)
        key_rot_grad = jnp.einsum('hts,htf->sf', score_low, query_rot)
        key_grad = rotate(key_rot_grad, cos_table, -sin_table).astype(jnp.bfloat16)
        value_grad = jnp.einsum('hts,htf->sf', probs_low, out_slice).astype(jnp.bfloat16)
        normed_grad = normed_grad + jnp.einsum('htf,hdf->td', query_grad.astype(jnp.float32), w_query.astype(jnp.float32))
        normed_grad = normed_grad + jnp.dot(key_grad, w_key.T, preferred_element_type=jnp.float32)
        normed_grad = normed_grad + jnp.dot(value_grad, w_value.T, preferred_element_type=jnp.float32)
        cotangents = jnp.stack([query_grad[0], key_grad, query_grad[1], value_grad]).astype(jnp.float32)
        per_slab = jnp.einsum('std,cstf->csdf', slab_normed, cotangents.reshape(4, N_SEQ, TOK_DEV, HD))
        weight_grads = lax.optimization_barrier(jnp.sum(rounded(per_slab), axis=1)).astype(jnp.bfloat16)
        return (normed_grad, (head_out, weight_grads))
    normed_grad, (head_out, weight_grads) = lax.scan(group, jnp.zeros((TOKENS, D), jnp.float32), jnp.arange(HEADS // 2, dtype=jnp.int32))
    attn_out = head_out.reshape(HEADS, TOKENS, HD).transpose(1, 0, 2).reshape(TOKENS, HEADS * HD)
    grad_table = weight_grads.reshape(HEADS * 2 * RB, BLK, BLK)
    padded = jnp.concatenate([grad_table, jnp.zeros((1, BLK, BLK), jnp.bfloat16)], axis=0)
    block_grads = padded[block_target].reshape(N_WT, SLOTS, BLK, BLK)
    scaled_grad = normed_grad * norm_gain[None, :]
    mean_prod = lax.optimization_barrier(jnp.mean(scaled_grad * scaled, axis=1))
    tokens_grad = (inv_rms[:, None] * (scaled_grad - scaled * mean_prod[:, None])).astype(jnp.bfloat16)
    gain_slab = lax.optimization_barrier(jnp.sum((normed_grad * scaled).reshape(N_SEQ, TOK_DEV, D), axis=1))
    gain_grad = lax.optimization_barrier(jnp.sum(rounded(gain_slab), axis=0))
    return (attn_out, tokens_grad, gain_grad, block_grads)
```

```python
import functools
import jax
import jax.numpy as jnp
from jax import lax
from jax.experimental import pallas as pl
from jax.experimental.pallas import tpu as pltpu
from jax.sharding import PartitionSpec as P

D = 4608
HD = 128
BLK = 128
CAP = 2
RB = D // BLK
POS = 2 * RB
TP = 256

query_scale = 144.0 ** (-0.5)
soft_cap = 50.0
norm_eps = 1e-06

MESH = pl.DeviceIdType.MESH
F32 = jnp.float32
BF16 = jnp.bfloat16


def dot(left, right, ldim, rdim):
    return lax.dot_general(
        left, right, (((ldim,), (rdim,)), ((), ())), preferred_element_type=F32
    )


def rot(v, c, s):
    return v * c + jnp.concatenate([v[:, HD // 2 :], v[:, : HD // 2]], axis=1) * s


def kernel(
    n_seq, n_wt,
    tok, gain, pos, cos, sin, blocks, slot_of, dest, place, og,
    attn, tg, gg, bg,
    tf, tokT, scT, ngT, sq, rd, nT, stage, arrived, arrp, invv, inv_sm, arrp_sm, wd, proj,
    kv, kvs, kvr, cot, wz, wzr, ws, fin, gs, gr, gb, nblk,
    sq_s, sq_r, pc_s, pc_r, bl_s, bl_r, nt_s, nt_r, kv_s, kv_r, kg_s, kg_r,
    wz_s, wz_r, ow_s, ow_r, fi_s, fi_r, g_s, g_r, rd_s, rd_r, gb_s, gb_r, loc,
):
    t_rows, feats = tok.shape
    slots = blocks.shape[0]
    fp = tf.shape[1]
    count = n_wt * CAP
    reach = n_seq // 2
    window = reach * t_rows
    chunk = CAP * BLK // n_seq
    z = lax.axis_index("seq")
    w = lax.axis_index("wt")
    par = lax.rem(w, 2)
    even = par == 0
    partner = w + 1 - 2 * par
    c_tab = cos[...]
    s_tab = sin[...]
    pending = []

    def send(src, dst, ss, rs, device):
        copy = pltpu.make_async_remote_copy(
            src_ref=src, dst_ref=dst, send_sem=ss, recv_sem=rs, device_id=device, device_id_type=MESH
        )
        copy.start()
        return copy

    def recv(dst, ss, rs):
        pltpu.make_async_remote_copy(
            src_ref=dst, dst_ref=dst, send_sem=ss, recv_sem=rs, device_id=(z, partner), device_id_type=MESH
        ).wait_recv()

    def to_wt(d):
        return lax.rem(w + d, n_wt)

    def from_wt(d):
        return lax.rem(w + n_wt - d, n_wt)

    def to_seq(d):
        return lax.rem(z + d, n_seq)

    def from_seq(d):
        return lax.rem(z + n_seq - d, n_seq)

    def frows(index):
        return pl.ds(pl.multiple_of(index * feats, 16), feats)

    barrier = pltpu.get_barrier_semaphore()
    for d in range(1, n_wt):
        pl.semaphore_signal(barrier, inc=1, device_id=(z, to_wt(d)), device_id_type=MESH)
    for d in range(1, n_seq):
        for other in (w, partner):
            pl.semaphore_signal(barrier, inc=1, device_id=(to_seq(d), other), device_id_type=MESH)

    tf[...] = jnp.zeros_like(tf)
    tf[:t_rows, :feats] = tok[...].astype(F32)
    turned = tf[...].T
    tokT[...] = turned
    sq[0] = jnp.broadcast_to(jnp.sum(turned * turned, axis=0, keepdims=True), (8, TP))
    for k in range(count):
        stage[k] = blocks[slot_of[k]]
    pl.semaphore_wait(barrier, n_wt - 1 + 2 * (n_seq - 1))

    for d in range(1, n_wt):
        pending.append(send(sq.at[0], sq.at[d], sq_s.at[d], sq_r.at[d], (z, to_wt(d))))
    for d in range(1, n_wt):
        u = to_wt(d)
        pending.append(send(place.at[u], arrp.at[w], pc_s.at[d], pc_r.at[d], (z, u)))
    for d in range(1, n_wt):
        u = to_wt(d)
        pending.append(
            send(stage.at[pl.ds(u * CAP, CAP)], arrived.at[pl.ds(w * CAP + 1, CAP)], bl_s.at[d], bl_r.at[d], (z, u))
        )
    arrp[w] = place[w]
    arrived[0] = jnp.zeros((BLK, BLK), BF16)
    for r in range(CAP):
        arrived[w * CAP + 1 + r] = stage[w * CAP + r]

    for d in range(1, n_wt):
        recv(sq.at[d], sq_s.at[d], sq_r.at[d])
    total = sq[0]
    for d in range(1, n_wt):
        total = total + sq[d]
    inv_row = lax.rsqrt(total / D + norm_eps)[0:1, :]
    scaled = tokT[:feats, :] * inv_row
    scT[...] = scaled
    nT[frows(w), :] = (scaled * gain[...]).astype(BF16)
    for d in range(1, n_wt):
        pending.append(send(nT.at[frows(w)], nT.at[frows(w)], nt_s.at[d], nt_r.at[d], (z, to_wt(d))))

    for d in range(1, n_wt):
        recv(arrp.at[from_wt(d)], pc_s.at[d], pc_r.at[d])
    lane = lax.broadcasted_iota(jnp.int32, (8, 128), 1)
    index = jnp.zeros((8, 128), jnp.int32)
    for o in range(n_wt):
        for r in range(CAP):
            index = jnp.where(arrp[o, r : r + 1, :] == lane, o * CAP + r + 1, index)
    invv[...] = index
    one = pltpu.make_async_copy(invv, inv_sm, loc.at[0])
    two = pltpu.make_async_copy(arrp, arrp_sm, loc.at[1])
    one.start()
    two.start()
    one.wait()
    two.wait()
    for d in range(1, n_wt):
        recv(arrived.at[pl.ds(from_wt(d) * CAP + 1, CAP)], bl_s.at[d], bl_r.at[d])
    for p in range(RB):
        wd[p * BLK : (p + 1) * BLK, :BLK] = arrived[inv_sm[0, p]]
        wd[p * BLK : (p + 1) * BLK, BLK:] = arrived[inv_sm[0, RB + p]]

    proj[...] = dot(nT[frows(w), :], wd[frows(w), :], 0, 0)
    for d in range(1, n_wt):
        src = from_wt(d)
        recv(nT.at[frows(src)], nt_s.at[d], nt_r.at[d])
        proj[...] += dot(nT[frows(src), :], wd[frows(src), :], 0, 0)

    query = (rot(proj[:t_rows, :HD], c_tab, s_tab) * query_scale).astype(BF16)
    pair = proj[:t_rows, HD:]
    kv[0, par] = jnp.where(even, rot(pair, c_tab, s_tab), pair).astype(BF16)

    kv_out = []

    def kv_send(off, which):
        device = (z + off, w if which == 0 else partner)
        return pltpu.make_async_remote_copy(
            src_ref=kv.at[0, par], dst_ref=kv.at[off, par], send_sem=kv_s.at[off * 2 + which],
            recv_sem=kv_r.at[off * 2 + which], device_id=device, device_id_type=MESH,
        )

    pending.append(kv_send(0, 1))
    pending[-1].start()
    for off in range(1, reach + 1):

        @pl.when(z + off < n_seq)
        def _():
            kv_send(off, 0).start()
            kv_send(off, 1).start()

        @pl.when(z < off)
        def _():
            kv[off] = jnp.zeros((2, t_rows, HD), BF16)

    for p in range(RB):
        nblk[p] = nT[p * BLK : (p + 1) * BLK, :]
    fin[n_seq * n_wt] = jnp.zeros((chunk, BLK), BF16)
    out_grad = og[...]
    recv(kv.at[0, 1 - par], kv_s.at[1], kv_r.at[1])
    for off in range(1, reach + 1):

        @pl.when(z >= off)
        def _():
            recv(kv.at[off, par], kv_s.at[off * 2], kv_r.at[off * 2])
            recv(kv.at[off, 1 - par], kv_s.at[off * 2 + 1], kv_r.at[off * 2 + 1])

    gap = lax.broadcasted_iota(jnp.int32, (t_rows, t_rows), 0) - lax.broadcasted_iota(
        jnp.int32, (t_rows, t_rows), 1
    )
    limit = jnp.minimum(pos[...], window - 1)
    exps, tanhs = [], []
    row_total = jnp.zeros((t_rows, 1), F32)
    mixed = jnp.zeros((t_rows, HD), F32)
    for off in range(reach + 1):
        t = jnp.tanh(dot(query, kv[off, 0], 1, 1) / soft_cap)
        far = gap + off * t_rows
        e = jnp.where((far >= 0) & (far <= limit), jnp.exp(soft_cap * t), 0.0)
        exps.append(e)
        tanhs.append(t)
        row_total = row_total + jnp.sum(e, axis=1, keepdims=True)
        mixed = mixed + dot(e.astype(BF16), kv[off, 1], 1, 0)
    inv_total = 1.0 / row_total
    attn_rows = (mixed * inv_total).astype(BF16)
    attn[...] = attn_rows
    delta = jnp.sum(out_grad.astype(F32) * attn_rows.astype(F32), axis=1, keepdims=True)

    def kg_send(off, which):
        device = (z - off, w if which == 0 else partner)
        return pltpu.make_async_remote_copy(
            src_ref=kvs.at[off, which], dst_ref=kvr.at[off, which], send_sem=kg_s.at[off * 2 + which],
            recv_sem=kg_r.at[off * 2 + which], device_id=device, device_id_type=MESH,
        )

    rot_grad = jnp.zeros((t_rows, HD), F32)
    own = None
    for off in range(reach, -1, -1):
        probs = exps[off] * inv_total
        pg = dot(out_grad, kv[off, 1], 1, 1)
        low = (probs * (pg - delta) * (1.0 - tanhs[off] * tanhs[off])).astype(BF16)
        rot_grad = rot_grad + dot(low, kv[off, 0], 1, 0)
        key_g = dot(low, query, 0, 0)
        val_g = dot(probs.astype(BF16), out_grad, 0, 0)
        own = jnp.where(even, key_g, val_g)
        kvs[off, 1] = jnp.where(even, val_g, key_g).astype(BF16)
        if off == 0:
            pending.append(kg_send(0, 1))
            pending[-1].start()
        else:
            kvs[off, 0] = own.astype(BF16)

            @pl.when(z >= off)
            def _():
                kg_send(off, 0).start()
                kg_send(off, 1).start()

            @pl.when(z + off >= n_seq)
            def _():
                kvr[off] = jnp.zeros((2, t_rows, HD), BF16)

    cot[...] = jnp.zeros_like(cot)
    cot[:t_rows, :HD] = (rot(rot_grad, c_tab, -s_tab) * query_scale).astype(BF16)
    recv(kvr.at[0, 1], kg_s.at[1], kg_r.at[1])
    own = own + kvr[0, 1].astype(F32)
    for off in range(1, reach + 1):

        @pl.when(z + off < n_seq)
        def _():
            recv(kvr.at[off, 0], kg_s.at[off * 2], kg_r.at[off * 2])
            recv(kvr.at[off, 1], kg_s.at[off * 2 + 1], kg_r.at[off * 2 + 1])

        own = own + kvr[off, 0].astype(F32) + kvr[off, 1].astype(F32)
    cot[:t_rows, HD:] = jnp.where(even, rot(own, c_tab, -s_tab), own).astype(BF16)

    for o in range(n_wt):
        for r in range(CAP):
            g = dot(nblk[arrp_sm[o, CAP + r, 0]], cot[...], 1, 0)
            g = jnp.where(arrp[o, r : r + 1, :] >= RB, g[:, BLK:], g[:, :BLK]).astype(BF16)
            for j in range(BLK // chunk):
                wz[r * (BLK // chunk) + j, o * chunk : (o + 1) * chunk, :] = g[j * chunk : (j + 1) * chunk]
    for d in range(1, n_seq):
        pending.append(send(wz.at[to_seq(d)], wzr.at[d], wz_s.at[d], wz_r.at[d], (to_seq(d), w)))

    for d in range(1, n_wt):
        o = to_wt(d)
        gs[frows(o), :] = dot(wd[frows(o), :], cot[...], 1, 1).astype(BF16)
        pending.append(send(gs.at[frows(o)], gr.at[d], g_s.at[d], g_r.at[d], (z, o)))
    ngT[...] = dot(wd[frows(w), :], cot[...], 1, 1)

    part = wz[z].astype(F32)
    for d in range(1, n_seq):
        recv(wzr.at[d], wz_s.at[d], wz_r.at[d])
        part = part + wzr[d].astype(F32)
    ws[...] = part.astype(BF16)

    def crows(i):
        return pl.ds(pl.multiple_of(i * chunk, 16), chunk)

    for d in range(1, n_wt):
        o = to_wt(d)
        pending.append(send(ws.at[crows(o)], fin.at[z * n_wt + w], ow_s.at[d], ow_r.at[d], (z, o)))
    fin[z * n_wt + w] = ws[crows(w), :]

    for d in range(1, n_wt):
        recv(gr.at[d], g_s.at[d], g_r.at[d])
        ngT[...] += gr[d].astype(F32)
    weighted = ngT[...] * scT[...]
    rd[0] = jnp.broadcast_to(jnp.sum(weighted * gain[...], axis=0, keepdims=True), (8, TP))
    for d in range(1, n_wt):
        pending.append(send(rd.at[0], rd.at[d], rd_s.at[d], rd_r.at[d], (z, to_wt(d))))

    for d in range(1, n_wt):
        recv(fin.at[z * n_wt + from_wt(d)], ow_s.at[d], ow_r.at[d])
    for d in range(1, n_seq):
        pending.append(send(fin.at[pl.ds(z * n_wt, n_wt)], fin.at[pl.ds(z * n_wt, n_wt)], fi_s.at[d], fi_r.at[d], (to_seq(d), w)))

    tokT[:feats, :128] = jnp.broadcast_to(jnp.sum(weighted, axis=1, keepdims=True), (feats, 128))
    gb[0] = tokT[:, :128].T[:8, :].astype(BF16).astype(F32)
    for d in range(1, n_seq):
        pending.append(send(gb.at[0], gb.at[d], gb_s.at[d], gb_r.at[d], (to_seq(d), w)))

    for d in range(1, n_wt):
        recv(rd.at[d], rd_s.at[d], rd_r.at[d])
    dots = rd[0]
    for d in range(1, n_wt):
        dots = dots + rd[d]
    dots_row = dots[0:1, :] / D
    tokT[:feats, :] = inv_row * (ngT[...] * gain[...] - scT[...] * dots_row)
    tg[...] = tokT[...].T[:t_rows, :feats].astype(BF16)

    for d in range(1, n_seq):
        recv(gb.at[d], gb_s.at[d], gb_r.at[d])
    sums = gb[0]
    for d in range(1, n_seq):
        sums = sums + gb[d]
    gg[...] = sums

    for d in range(1, n_seq):
        recv(fin.at[pl.ds(from_seq(d) * n_wt, n_wt)], fi_s.at[d], fi_r.at[d])
    per = BLK // chunk
    for s in range(slots):
        for j in range(per):
            bg[s, j * chunk : (j + 1) * chunk, :] = fin[dest[s * per + j]]

    for copy in pending:
        copy.wait_send()
    for off in range(1, reach + 1):

        @pl.when(z + off < n_seq)
        def _():
            kv_send(off, 0).wait_send()
            kv_send(off, 1).wait_send()

        @pl.when(z >= off)
        def _():
            kg_send(off, 0).wait_send()
            kg_send(off, 1).wait_send()


def body(tokens_in, norm_gain, positions, blocks, slot_code, out_grad):
    t_rows, feats = tokens_in.shape
    n_wt = lax.axis_size("wt")
    n_seq = lax.axis_size("seq")
    slots = blocks.shape[1]
    count = n_wt * CAP
    reach = n_seq // 2
    chunk = CAP * BLK // n_seq
    fp = -(-feats // 128) * 128
    half = HD // 2
    frequency = 10000.0 ** (-2.0 * jnp.arange(half, dtype=F32) / HD)
    angles = positions.astype(F32)[:, None] * frequency[None, :]
    cos, sin = jnp.cos(angles), jnp.sin(angles)
    cos = jnp.concatenate([cos, cos], axis=1)
    sin = jnp.concatenate([-sin, sin], axis=1)
    codes = slot_code[0]
    live = codes >= 0
    user = jnp.where(live, codes // POS, -1)
    ids = jnp.arange(slots, dtype=jnp.int32)
    before = (user[None, :] == user[:, None]) & (ids[None, :] < ids[:, None])
    rank = jnp.sum(before.astype(jnp.int32), axis=1)
    dest = jnp.where(live, user * CAP + rank, -1)
    hit = dest[None, :] == jnp.arange(count, dtype=jnp.int32)[:, None]
    slot_of = jnp.sum(jnp.where(hit, ids[None, :], 0), axis=1)
    spot = jnp.sum(jnp.where(hit, (codes - user * POS + 1)[None, :], 0), axis=1) - 1
    spot = spot.reshape(n_wt, CAP)
    row = jnp.maximum(jnp.where(spot >= RB, spot - RB, spot), 0)
    place = jnp.concatenate([spot, row, jnp.zeros((n_wt, 8 - 2 * CAP), jnp.int32)], axis=1)
    place = jnp.broadcast_to(place[:, :, None], (n_wt, 8, 128))
    per = BLK // chunk
    piece = (rank[:, None] * per + jnp.arange(per, dtype=jnp.int32)[None, :]) * n_wt + user[:, None]
    piece = jnp.where(live[:, None], piece, n_seq * n_wt).reshape(-1)
    vmem = pl.BlockSpec(memory_space=pltpu.VMEM)
    smem = pl.BlockSpec(memory_space=pltpu.SMEM)
    dma = lambda n: pltpu.SemaphoreType.DMA((n,))
    kvn = 2 * (reach + 1)
    attn, tg, gg, bg = pl.pallas_call(
        functools.partial(kernel, n_seq, n_wt),
        out_shape=(
            jax.ShapeDtypeStruct((t_rows, HD), BF16),
            jax.ShapeDtypeStruct((t_rows, feats), BF16),
            jax.ShapeDtypeStruct((8, fp), F32),
            jax.ShapeDtypeStruct((slots, BLK, BLK), BF16),
        ),
        in_specs=[vmem] * 6 + [smem] * 2 + [vmem] * 2,
        out_specs=(vmem,) * 4,
        scratch_shapes=[
            pltpu.VMEM((TP, fp), F32),
            pltpu.VMEM((fp, TP), F32),
            pltpu.VMEM((feats, TP), F32),
            pltpu.VMEM((feats, TP), F32),
            pltpu.VMEM((n_wt, 8, TP), F32),
            pltpu.VMEM((n_wt, 8, TP), F32),
            pltpu.VMEM((D, TP), BF16),
            pltpu.VMEM((count, BLK, BLK), BF16),
            pltpu.VMEM((count + 1, BLK, BLK), BF16),
            pltpu.VMEM((n_wt, 8, 128), jnp.int32),
            pltpu.VMEM((8, 128), jnp.int32),
            pltpu.SMEM((8, 128), jnp.int32),
            pltpu.SMEM((n_wt, 8, 128), jnp.int32),
            pltpu.VMEM((D, 2 * HD), BF16),
            pltpu.VMEM((TP, 2 * HD), F32),
            pltpu.VMEM((reach + 1, 2, t_rows, HD), BF16),
            pltpu.VMEM((reach + 1, 2, t_rows, HD), BF16),
            pltpu.VMEM((reach + 1, 2, t_rows, HD), BF16),
            pltpu.VMEM((TP, 2 * HD), BF16),
            pltpu.VMEM((n_seq, n_wt * chunk, BLK), BF16),
            pltpu.VMEM((n_seq, n_wt * chunk, BLK), BF16),
            pltpu.VMEM((n_wt * chunk, BLK), BF16),
            pltpu.VMEM((n_seq * n_wt + 1, chunk, BLK), BF16),
            pltpu.VMEM((D, TP), BF16),
            pltpu.VMEM((n_wt, feats, TP), BF16),
            pltpu.VMEM((n_seq, 8, fp), F32),
            pltpu.VMEM((RB, BLK, TP), BF16),
        ]
        + [dma(n_wt)] * 8
        + [dma(kvn)] * 4
        + [dma(n_seq)] * 2
        + [dma(n_wt)] * 2
        + [dma(n_seq)] * 2
        + [dma(n_wt)] * 4
        + [dma(n_seq)] * 2
        + [dma(2)],
        compiler_params=pltpu.CompilerParams(
            collective_id=0, has_side_effects=True, vmem_limit_bytes=56 * 1024 * 1024
        ),
    )(
        tokens_in, norm_gain[:, None], positions[:, None], cos, sin, blocks[0],
        slot_of.astype(jnp.int32), piece.astype(jnp.int32), place.astype(jnp.int32), out_grad,
    )
    return attn, tg, gg[0, :feats], bg[None]


def solution(mesh):
    placed = (
        P("seq", "wt"),
        P("wt"),
        P("seq"),
        P("wt", None, None, None),
        P("wt", None),
        P("seq", "wt"),
    )
    return jax.shard_map(
        body,
        mesh=mesh,
        in_specs=placed,
        out_specs=(P("seq", "wt"), P("seq", "wt"), P("wt"), P("wt", None, None, None)),
        check_vma=False,
    )
```

```python
import functools
import jax
import jax.numpy as jnp
from jax import lax
from jax.experimental import pallas as pl
from jax.experimental.pallas import tpu as pltpu
from jax.sharding import PartitionSpec as P

D = 4608
HD = 128
BLK = 128
CAP = 2
RB = D // BLK
POS = 2 * RB
TP = 256

query_scale = 144.0 ** (-0.5)
soft_cap = 50.0
norm_eps = 1e-06

MESH = pl.DeviceIdType.MESH
F32 = jnp.float32
BF16 = jnp.bfloat16


def dot(left, right, ldim, rdim):
    return lax.dot_general(
        left, right, (((ldim,), (rdim,)), ((), ())), preferred_element_type=F32
    )


def rot(v, c, s):
    return v * c + jnp.concatenate([v[:, HD // 2 :], v[:, : HD // 2]], axis=1) * s


def kernel(
    n_seq, n_wt,
    tok, gain, pos, cos, sin, blocks, slot_of, dest, place, og,
    attn, tg, gg, bg,
    tf, tokT, scT, ngT, sq, rd, nT, stage, arrived, arrp, invv, inv_sm, arrp_sm, wd, proj,
    kv, kvs, kvr, cot, wz, wzr, ws, fin, gs, gr, gb, nblk,
    sq_s, sq_r, pc_s, pc_r, bl_s, bl_r, nt_s, nt_r, kv_s, kv_r, kg_s, kg_r,
    wz_s, wz_r, ow_s, ow_r, fi_s, fi_r, g_s, g_r, rd_s, rd_r, gb_s, gb_r, loc,
):
    t_rows, feats = tok.shape
    slots = blocks.shape[0]
    fp = tf.shape[1]
    count = n_wt * CAP
    reach = n_seq // 2
    window = reach * t_rows
    chunk = CAP * BLK // n_seq
    z = lax.axis_index("seq")
    w = lax.axis_index("wt")
    par = lax.rem(w, 2)
    even = par == 0
    partner = w + 1 - 2 * par
    c_tab = cos[...]
    s_tab = sin[...]
    pending = []

    def send(src, dst, ss, rs, device):
        copy = pltpu.make_async_remote_copy(
            src_ref=src, dst_ref=dst, send_sem=ss, recv_sem=rs, device_id=device, device_id_type=MESH
        )
        copy.start()
        return copy

    def recv(dst, ss, rs):
        pltpu.make_async_remote_copy(
            src_ref=dst, dst_ref=dst, send_sem=ss, recv_sem=rs, device_id=(z, partner), device_id_type=MESH
        ).wait_recv()

    def to_wt(d):
        return lax.rem(w + d, n_wt)

    def from_wt(d):
        return lax.rem(w + n_wt - d, n_wt)

    def to_seq(d):
        return lax.rem(z + d, n_seq)

    def from_seq(d):
        return lax.rem(z + n_seq - d, n_seq)

    def frows(index):
        return pl.ds(pl.multiple_of(index * feats, 16), feats)

    barrier = pltpu.get_barrier_semaphore()
    for d in range(1, n_wt):
        pl.semaphore_signal(barrier, inc=1, device_id=(z, to_wt(d)), device_id_type=MESH)
    for d in range(1, n_seq):
        for other in (w, partner):
            pl.semaphore_signal(barrier, inc=1, device_id=(to_seq(d), other), device_id_type=MESH)

    tf[...] = jnp.zeros_like(tf)
    tf[:t_rows, :feats] = tok[...].astype(F32)
    turned = tf[...].T
    tokT[...] = turned
    sq[0] = jnp.broadcast_to(jnp.sum(turned * turned, axis=0, keepdims=True), (8, TP))
    for k in range(count):
        stage[k] = blocks[slot_of[k]]
    pl.semaphore_wait(barrier, n_wt - 1 + 2 * (n_seq - 1))

    for d in range(1, n_wt):
        pending.append(send(sq.at[0], sq.at[d], sq_s.at[d], sq_r.at[d], (z, to_wt(d))))
    for d in range(1, n_wt):
        u = to_wt(d)
        pending.append(send(place.at[u], arrp.at[w], pc_s.at[d], pc_r.at[d], (z, u)))
    for d in range(1, n_wt):
        u = to_wt(d)
        pending.append(
            send(stage.at[pl.ds(u * CAP, CAP)], arrived.at[pl.ds(w * CAP + 1, CAP)], bl_s.at[d], bl_r.at[d], (z, u))
        )
    arrp[w] = place[w]
    arrived[0] = jnp.zeros((BLK, BLK), BF16)
    for r in range(CAP):
        arrived[w * CAP + 1 + r] = stage[w * CAP + r]

    for d in range(1, n_wt):
        recv(sq.at[d], sq_s.at[d], sq_r.at[d])
    total = sq[0]
    for d in range(1, n_wt):
        total = total + sq[d]
    inv_row = lax.rsqrt(total / D + norm_eps)[0:1, :]
    scaled = tokT[:feats, :] * inv_row
    scT[...] = scaled
    nT[frows(w), :] = (scaled * gain[...]).astype(BF16)
    for d in [*range(2, n_wt, 2), 1]:
        device = (z, partner) if d == 1 else (z, to_wt(d))
        pending.append(send(nT.at[frows(w)], nT.at[frows(w)], nt_s.at[d], nt_r.at[d], device))

    for d in range(1, n_wt):
        recv(arrp.at[from_wt(d)], pc_s.at[d], pc_r.at[d])
    lane = lax.broadcasted_iota(jnp.int32, (8, 128), 1)
    index = jnp.zeros((8, 128), jnp.int32)
    for o in range(n_wt):
        for r in range(CAP):
            index = jnp.where(arrp[o, r : r + 1, :] == lane, o * CAP + r + 1, index)
    invv[...] = index
    one = pltpu.make_async_copy(invv, inv_sm, loc.at[0])
    two = pltpu.make_async_copy(arrp, arrp_sm, loc.at[1])
    one.start()
    two.start()
    one.wait()
    two.wait()
    for d in range(1, n_wt):
        recv(arrived.at[pl.ds(from_wt(d) * CAP + 1, CAP)], bl_s.at[d], bl_r.at[d])
    for p in range(RB):
        wd[p * BLK : (p + 1) * BLK, :BLK] = arrived[inv_sm[0, p]]
        wd[p * BLK : (p + 1) * BLK, BLK:] = arrived[inv_sm[0, RB + p]]

    proj[...] = dot(nT[frows(w), :], wd[frows(w), :], 0, 0)

    def add_proj(src):
        proj[...] += dot(nT[frows(src), :], wd[frows(src), :], 0, 0)

    recv(nT.at[frows(partner)], nt_s.at[1], nt_r.at[1])
    add_proj(partner)
    for d in range(2, n_wt, 2):
        src = from_wt(d)
        recv(nT.at[frows(src)], nt_s.at[d], nt_r.at[d])
        pending.append(send(nT.at[frows(src)], nT.at[frows(src)], nt_s.at[d + 1], nt_r.at[d + 1], (z, partner)))
        add_proj(src)
    for d in range(2, n_wt, 2):
        src = lax.rem(partner + n_wt - d, n_wt)
        recv(nT.at[frows(src)], nt_s.at[d + 1], nt_r.at[d + 1])
        add_proj(src)

    query = (rot(proj[:t_rows, :HD], c_tab, s_tab) * query_scale).astype(BF16)
    pair = proj[:t_rows, HD:]
    kv[0, par] = jnp.where(even, rot(pair, c_tab, s_tab), pair).astype(BF16)

    kv_out = []

    def kv_send(off, which):
        device = (z + off, w if which == 0 else partner)
        return pltpu.make_async_remote_copy(
            src_ref=kv.at[0, par], dst_ref=kv.at[off, par], send_sem=kv_s.at[off * 2 + which],
            recv_sem=kv_r.at[off * 2 + which], device_id=device, device_id_type=MESH,
        )

    pending.append(kv_send(0, 1))
    pending[-1].start()
    for off in range(1, reach + 1):

        @pl.when(z + off < n_seq)
        def _():
            kv_send(off, 0).start()
            kv_send(off, 1).start()

        @pl.when(z < off)
        def _():
            kv[off] = jnp.zeros((2, t_rows, HD), BF16)

    for p in range(RB):
        nblk[p] = nT[p * BLK : (p + 1) * BLK, :]
    fin[n_seq * n_wt] = jnp.zeros((chunk, BLK), BF16)
    out_grad = og[...]
    recv(kv.at[0, 1 - par], kv_s.at[1], kv_r.at[1])
    for off in range(1, reach + 1):

        @pl.when(z >= off)
        def _():
            recv(kv.at[off, par], kv_s.at[off * 2], kv_r.at[off * 2])
            recv(kv.at[off, 1 - par], kv_s.at[off * 2 + 1], kv_r.at[off * 2 + 1])

    gap = lax.broadcasted_iota(jnp.int32, (t_rows, t_rows), 0) - lax.broadcasted_iota(
        jnp.int32, (t_rows, t_rows), 1
    )
    limit = jnp.minimum(pos[...], window - 1)
    exps, tanhs = [], []
    row_total = jnp.zeros((t_rows, 1), F32)
    mixed = jnp.zeros((t_rows, HD), F32)
    for off in range(reach + 1):
        t = jnp.tanh(dot(query, kv[off, 0], 1, 1) / soft_cap)
        far = gap + off * t_rows
        e = jnp.where((far >= 0) & (far <= limit), jnp.exp(soft_cap * t), 0.0)
        exps.append(e)
        tanhs.append(t)
        row_total = row_total + jnp.sum(e, axis=1, keepdims=True)
        mixed = mixed + dot(e.astype(BF16), kv[off, 1], 1, 0)
    inv_total = 1.0 / row_total
    attn_rows = (mixed * inv_total).astype(BF16)
    attn[...] = attn_rows
    delta = jnp.sum(out_grad.astype(F32) * attn_rows.astype(F32), axis=1, keepdims=True)

    def kg_send(off, which):
        device = (z - off, w if which == 0 else partner)
        return pltpu.make_async_remote_copy(
            src_ref=kvs.at[off, which], dst_ref=kvr.at[off, which], send_sem=kg_s.at[off * 2 + which],
            recv_sem=kg_r.at[off * 2 + which], device_id=device, device_id_type=MESH,
        )

    rot_grad = jnp.zeros((t_rows, HD), F32)
    own = None
    for off in range(reach, -1, -1):
        probs = exps[off] * inv_total
        pg = dot(out_grad, kv[off, 1], 1, 1)
        low = (probs * (pg - delta) * (1.0 - tanhs[off] * tanhs[off])).astype(BF16)
        rot_grad = rot_grad + dot(low, kv[off, 0], 1, 0)
        key_g = dot(low, query, 0, 0)
        val_g = dot(probs.astype(BF16), out_grad, 0, 0)
        own = jnp.where(even, key_g, val_g)
        kvs[off, 1] = jnp.where(even, val_g, key_g).astype(BF16)
        if off == 0:
            pending.append(kg_send(0, 1))
            pending[-1].start()
        else:
            kvs[off, 0] = own.astype(BF16)

            @pl.when(z >= off)
            def _():
                kg_send(off, 0).start()
                kg_send(off, 1).start()

            @pl.when(z + off >= n_seq)
            def _():
                kvr[off] = jnp.zeros((2, t_rows, HD), BF16)

    cot[...] = jnp.zeros_like(cot)
    cot[:t_rows, :HD] = (rot(rot_grad, c_tab, -s_tab) * query_scale).astype(BF16)
    recv(kvr.at[0, 1], kg_s.at[1], kg_r.at[1])
    own = own + kvr[0, 1].astype(F32)
    for off in range(1, reach + 1):

        @pl.when(z + off < n_seq)
        def _():
            recv(kvr.at[off, 0], kg_s.at[off * 2], kg_r.at[off * 2])
            recv(kvr.at[off, 1], kg_s.at[off * 2 + 1], kg_r.at[off * 2 + 1])

        own = own + kvr[off, 0].astype(F32) + kvr[off, 1].astype(F32)
    cot[:t_rows, HD:] = jnp.where(even, rot(own, c_tab, -s_tab), own).astype(BF16)

    for o in range(n_wt):
        for r in range(CAP):
            g = dot(nblk[arrp_sm[o, CAP + r, 0]], cot[...], 1, 0)
            g = jnp.where(arrp[o, r : r + 1, :] >= RB, g[:, BLK:], g[:, :BLK]).astype(BF16)
            for j in range(BLK // chunk):
                wz[r * (BLK // chunk) + j, o * chunk : (o + 1) * chunk, :] = g[j * chunk : (j + 1) * chunk]
    for d in range(1, n_seq):
        pending.append(send(wz.at[to_seq(d)], wzr.at[d], wz_s.at[d], wz_r.at[d], (to_seq(d), w)))

    order = [*range(2, n_wt, 2), 0]
    for d in order:
        o = lax.rem(partner + d, n_wt)
        gs[frows(o), :] = dot(wd[frows(o), :], cot[...], 1, 1).astype(BF16)
        pending.append(send(gs.at[frows(o)], gr.at[d + 1], g_s.at[d + 1], g_r.at[d + 1], (z, partner)))
    for d in order:
        o = to_wt(d)
        g = dot(wd[frows(o), :], cot[...], 1, 1)
        recv(gr.at[d + 1], g_s.at[d + 1], g_r.at[d + 1])
        g = g + gr[d + 1].astype(F32)
        if d == 0:
            ngT[...] = g
        else:
            gs[frows(o), :] = g.astype(BF16)
            pending.append(send(gs.at[frows(o)], gr.at[d], g_s.at[d], g_r.at[d], (z, o)))

    part = wz[z].astype(F32)
    for d in range(1, n_seq):
        recv(wzr.at[d], wz_s.at[d], wz_r.at[d])
        part = part + wzr[d].astype(F32)
    ws[...] = part.astype(BF16)

    def crows(i):
        return pl.ds(pl.multiple_of(i * chunk, 16), chunk)

    for d in range(1, n_wt):
        o = to_wt(d)
        pending.append(send(ws.at[crows(o)], fin.at[z * n_wt + w], ow_s.at[d], ow_r.at[d], (z, o)))
    fin[z * n_wt + w] = ws[crows(w), :]

    for d in range(2, n_wt, 2):
        recv(gr.at[d], g_s.at[d], g_r.at[d])
        ngT[...] += gr[d].astype(F32)
    weighted = ngT[...] * scT[...]
    rd[0] = jnp.broadcast_to(jnp.sum(weighted * gain[...], axis=0, keepdims=True), (8, TP))
    for d in range(1, n_wt):
        pending.append(send(rd.at[0], rd.at[d], rd_s.at[d], rd_r.at[d], (z, to_wt(d))))

    for d in range(1, n_wt):
        recv(fin.at[z * n_wt + from_wt(d)], ow_s.at[d], ow_r.at[d])
    for d in range(1, n_seq):
        pending.append(send(fin.at[pl.ds(z * n_wt, n_wt)], fin.at[pl.ds(z * n_wt, n_wt)], fi_s.at[d], fi_r.at[d], (to_seq(d), w)))

    tokT[:feats, :128] = jnp.broadcast_to(jnp.sum(weighted, axis=1, keepdims=True), (feats, 128))
    gb[0] = tokT[:, :128].T[:8, :].astype(BF16).astype(F32)
    for d in range(1, n_seq):
        pending.append(send(gb.at[0], gb.at[d], gb_s.at[d], gb_r.at[d], (to_seq(d), w)))

    for d in range(1, n_wt):
        recv(rd.at[d], rd_s.at[d], rd_r.at[d])
    dots = rd[0]
    for d in range(1, n_wt):
        dots = dots + rd[d]
    dots_row = dots[0:1, :] / D
    tokT[:feats, :] = inv_row * (ngT[...] * gain[...] - scT[...] * dots_row)
    tg[...] = tokT[...].T[:t_rows, :feats].astype(BF16)

    for d in range(1, n_seq):
        recv(gb.at[d], gb_s.at[d], gb_r.at[d])
    sums = gb[0]
    for d in range(1, n_seq):
        sums = sums + gb[d]
    gg[...] = sums

    for d in range(1, n_seq):
        recv(fin.at[pl.ds(from_seq(d) * n_wt, n_wt)], fi_s.at[d], fi_r.at[d])
    per = BLK // chunk
    for s in range(slots):
        for j in range(per):
            bg[s, j * chunk : (j + 1) * chunk, :] = fin[dest[s * per + j]]

    for copy in pending:
        copy.wait_send()
    for off in range(1, reach + 1):

        @pl.when(z + off < n_seq)
        def _():
            kv_send(off, 0).wait_send()
            kv_send(off, 1).wait_send()

        @pl.when(z >= off)
        def _():
            kg_send(off, 0).wait_send()
            kg_send(off, 1).wait_send()


def body(tokens_in, norm_gain, positions, blocks, slot_code, out_grad):
    t_rows, feats = tokens_in.shape
    n_wt = lax.axis_size("wt")
    n_seq = lax.axis_size("seq")
    slots = blocks.shape[1]
    count = n_wt * CAP
    reach = n_seq // 2
    chunk = CAP * BLK // n_seq
    fp = -(-feats // 128) * 128
    half = HD // 2
    frequency = 10000.0 ** (-2.0 * jnp.arange(half, dtype=F32) / HD)
    angles = positions.astype(F32)[:, None] * frequency[None, :]
    cos, sin = jnp.cos(angles), jnp.sin(angles)
    cos = jnp.concatenate([cos, cos], axis=1)
    sin = jnp.concatenate([-sin, sin], axis=1)
    codes = slot_code[0]
    live = codes >= 0
    user = jnp.where(live, codes // POS, -1)
    ids = jnp.arange(slots, dtype=jnp.int32)
    before = (user[None, :] == user[:, None]) & (ids[None, :] < ids[:, None])
    rank = jnp.sum(before.astype(jnp.int32), axis=1)
    dest = jnp.where(live, user * CAP + rank, -1)
    hit = dest[None, :] == jnp.arange(count, dtype=jnp.int32)[:, None]
    slot_of = jnp.sum(jnp.where(hit, ids[None, :], 0), axis=1)
    spot = jnp.sum(jnp.where(hit, (codes - user * POS + 1)[None, :], 0), axis=1) - 1
    spot = spot.reshape(n_wt, CAP)
    row = jnp.maximum(jnp.where(spot >= RB, spot - RB, spot), 0)
    place = jnp.concatenate([spot, row, jnp.zeros((n_wt, 8 - 2 * CAP), jnp.int32)], axis=1)
    place = jnp.broadcast_to(place[:, :, None], (n_wt, 8, 128))
    per = BLK // chunk
    piece = (rank[:, None] * per + jnp.arange(per, dtype=jnp.int32)[None, :]) * n_wt + user[:, None]
    piece = jnp.where(live[:, None], piece, n_seq * n_wt).reshape(-1)
    vmem = pl.BlockSpec(memory_space=pltpu.VMEM)
    smem = pl.BlockSpec(memory_space=pltpu.SMEM)
    dma = lambda n: pltpu.SemaphoreType.DMA((n,))
    kvn = 2 * (reach + 1)
    attn, tg, gg, bg = pl.pallas_call(
        functools.partial(kernel, n_seq, n_wt),
        out_shape=(
            jax.ShapeDtypeStruct((t_rows, HD), BF16),
            jax.ShapeDtypeStruct((t_rows, feats), BF16),
            jax.ShapeDtypeStruct((8, fp), F32),
            jax.ShapeDtypeStruct((slots, BLK, BLK), BF16),
        ),
        in_specs=[vmem] * 6 + [smem] * 2 + [vmem] * 2,
        out_specs=(vmem,) * 4,
        scratch_shapes=[
            pltpu.VMEM((TP, fp), F32),
            pltpu.VMEM((fp, TP), F32),
            pltpu.VMEM((feats, TP), F32),
            pltpu.VMEM((feats, TP), F32),
            pltpu.VMEM((n_wt, 8, TP), F32),
            pltpu.VMEM((n_wt, 8, TP), F32),
            pltpu.VMEM((D, TP), BF16),
            pltpu.VMEM((count, BLK, BLK), BF16),
            pltpu.VMEM((count + 1, BLK, BLK), BF16),
            pltpu.VMEM((n_wt, 8, 128), jnp.int32),
            pltpu.VMEM((8, 128), jnp.int32),
            pltpu.SMEM((8, 128), jnp.int32),
            pltpu.SMEM((n_wt, 8, 128), jnp.int32),
            pltpu.VMEM((D, 2 * HD), BF16),
            pltpu.VMEM((TP, 2 * HD), F32),
            pltpu.VMEM((reach + 1, 2, t_rows, HD), BF16),
            pltpu.VMEM((reach + 1, 2, t_rows, HD), BF16),
            pltpu.VMEM((reach + 1, 2, t_rows, HD), BF16),
            pltpu.VMEM((TP, 2 * HD), BF16),
            pltpu.VMEM((n_seq, n_wt * chunk, BLK), BF16),
            pltpu.VMEM((n_seq, n_wt * chunk, BLK), BF16),
            pltpu.VMEM((n_wt * chunk, BLK), BF16),
            pltpu.VMEM((n_seq * n_wt + 1, chunk, BLK), BF16),
            pltpu.VMEM((D, TP), BF16),
            pltpu.VMEM((n_wt, feats, TP), BF16),
            pltpu.VMEM((n_seq, 8, fp), F32),
            pltpu.VMEM((RB, BLK, TP), BF16),
        ]
        + [dma(n_wt)] * 8
        + [dma(kvn)] * 4
        + [dma(n_seq)] * 2
        + [dma(n_wt)] * 2
        + [dma(n_seq)] * 2
        + [dma(n_wt)] * 4
        + [dma(n_seq)] * 2
        + [dma(2)],
        compiler_params=pltpu.CompilerParams(
            collective_id=0, has_side_effects=True, vmem_limit_bytes=56 * 1024 * 1024
        ),
    )(
        tokens_in, norm_gain[:, None], positions[:, None], cos, sin, blocks[0],
        slot_of.astype(jnp.int32), piece.astype(jnp.int32), place.astype(jnp.int32), out_grad,
    )
    return attn, tg, gg[0, :feats], bg[None]


def solution(mesh):
    placed = (
        P("seq", "wt"),
        P("wt"),
        P("seq"),
        P("wt", None, None, None),
        P("wt", None),
        P("seq", "wt"),
    )
    return jax.shard_map(
        body,
        mesh=mesh,
        in_specs=placed,
        out_specs=(P("seq", "wt"), P("seq", "wt"), P("wt"), P("wt", None, None, None)),
        check_vma=False,
    )
```

```python
import functools
import jax
import jax.numpy as jnp
from jax import lax
from jax.experimental import pallas as pl
from jax.experimental.pallas import tpu as pltpu
from jax.sharding import PartitionSpec as P

D = 4608
HD = 128
BLK = 128
CAP = 2
RB = D // BLK
POS = 2 * RB
TP = 256

query_scale = 144.0 ** (-0.5)
soft_cap = 50.0
norm_eps = 1e-06

MESH = pl.DeviceIdType.MESH
F32 = jnp.float32
BF16 = jnp.bfloat16


def dot(left, right, ldim, rdim):
    return lax.dot_general(
        left, right, (((ldim,), (rdim,)), ((), ())), preferred_element_type=F32
    )


def rot(v, c, s):
    return v * c + jnp.concatenate([v[:, HD // 2 :], v[:, : HD // 2]], axis=1) * s


def kernel(
    n_seq, n_wt,
    tok, gain, pos, cos, sin, blocks, slot_of, dest, place, og,
    attn, tg, gg, bg,
    tf, tokT, scT, ngT, sq, rd, nT, stage, arrived, arrp, invv, inv_sm, arrp_sm, wd, proj,
    kv, kvs, kvr, cot, wz, wzr, ws, fin, gs, gr, gb, nblk,
    sq_s, sq_r, pc_s, pc_r, bl_s, bl_r, nt_s, nt_r, kv_s, kv_r, kg_s, kg_r,
    wz_s, wz_r, ow_s, ow_r, fi_s, fi_r, g_s, g_r, rd_s, rd_r, gb_s, gb_r, loc,
):
    t_rows, feats = tok.shape
    slots = blocks.shape[0]
    fp = tf.shape[1]
    count = n_wt * CAP
    reach = n_seq // 2
    window = reach * t_rows
    chunk = CAP * BLK // n_seq
    z = lax.axis_index("seq")
    w = lax.axis_index("wt")
    par = lax.rem(w, 2)
    even = par == 0
    partner = w + 1 - 2 * par
    c_tab = cos[...]
    s_tab = sin[...]
    pending = []

    def send(src, dst, ss, rs, device):
        copy = pltpu.make_async_remote_copy(
            src_ref=src, dst_ref=dst, send_sem=ss, recv_sem=rs, device_id=device, device_id_type=MESH
        )
        copy.start()
        return copy

    def recv(dst, ss, rs):
        pltpu.make_async_remote_copy(
            src_ref=dst, dst_ref=dst, send_sem=ss, recv_sem=rs, device_id=(z, partner), device_id_type=MESH
        ).wait_recv()

    def to_wt(d):
        return lax.rem(w + d, n_wt)

    def from_wt(d):
        return lax.rem(w + n_wt - d, n_wt)

    def to_seq(d):
        return lax.rem(z + d, n_seq)

    def from_seq(d):
        return lax.rem(z + n_seq - d, n_seq)

    def frows(index):
        return pl.ds(pl.multiple_of(index * feats, 16), feats)

    barrier = pltpu.get_barrier_semaphore()
    for d in range(1, n_wt):
        pl.semaphore_signal(barrier, inc=1, device_id=(z, to_wt(d)), device_id_type=MESH)
    for d in range(1, n_seq):
        for other in (w, partner):
            pl.semaphore_signal(barrier, inc=1, device_id=(to_seq(d), other), device_id_type=MESH)

    tf[...] = jnp.zeros_like(tf)
    tf[:t_rows, :feats] = tok[...].astype(F32)
    turned = tf[...].T
    tokT[...] = turned
    sq[0] = jnp.broadcast_to(jnp.sum(turned * turned, axis=0, keepdims=True), (8, TP))
    for k in range(count):
        stage[k] = blocks[slot_of[k]]
    pl.semaphore_wait(barrier, n_wt - 1 + 2 * (n_seq - 1))

    for d in range(1, n_wt):
        pending.append(send(sq.at[0], sq.at[d], sq_s.at[d], sq_r.at[d], (z, to_wt(d))))
    for d in range(1, n_wt):
        u = to_wt(d)
        pending.append(send(place.at[u], arrp.at[w], pc_s.at[d], pc_r.at[d], (z, u)))
    for d in range(1, n_wt):
        u = to_wt(d)
        pending.append(
            send(stage.at[pl.ds(u * CAP, CAP)], arrived.at[pl.ds(w * CAP + 1, CAP)], bl_s.at[d], bl_r.at[d], (z, u))
        )
    arrp[w] = place[w]
    arrived[0] = jnp.zeros((BLK, BLK), BF16)
    for r in range(CAP):
        arrived[w * CAP + 1 + r] = stage[w * CAP + r]

    for d in range(1, n_wt):
        recv(sq.at[d], sq_s.at[d], sq_r.at[d])
    total = sq[0]
    for d in range(1, n_wt):
        total = total + sq[d]
    inv_row = lax.rsqrt(total / D + norm_eps)[0:1, :]
    scaled = tokT[:feats, :] * inv_row
    scT[...] = scaled
    nT[frows(w), :] = (scaled * gain[...]).astype(BF16)
    for d in [*range(2, n_wt, 2), 1]:
        device = (z, partner) if d == 1 else (z, to_wt(d))
        pending.append(send(nT.at[frows(w)], nT.at[frows(w)], nt_s.at[d], nt_r.at[d], device))

    for d in range(1, n_wt):
        recv(arrp.at[from_wt(d)], pc_s.at[d], pc_r.at[d])
    lane = lax.broadcasted_iota(jnp.int32, (8, 128), 1)
    index = jnp.zeros((8, 128), jnp.int32)
    for o in range(n_wt):
        for r in range(CAP):
            index = jnp.where(arrp[o, r : r + 1, :] == lane, o * CAP + r + 1, index)
    invv[...] = index
    one = pltpu.make_async_copy(invv, inv_sm, loc.at[0])
    two = pltpu.make_async_copy(arrp, arrp_sm, loc.at[1])
    one.start()
    two.start()
    one.wait()
    two.wait()
    for d in range(1, n_wt):
        recv(arrived.at[pl.ds(from_wt(d) * CAP + 1, CAP)], bl_s.at[d], bl_r.at[d])
    for p in range(RB):
        wd[p * BLK : (p + 1) * BLK, :BLK] = arrived[inv_sm[0, p]]
        wd[p * BLK : (p + 1) * BLK, BLK:] = arrived[inv_sm[0, RB + p]]

    proj[...] = dot(nT[frows(w), :], wd[frows(w), :], 0, 0)

    def add_proj(src):
        proj[...] += dot(nT[frows(src), :], wd[frows(src), :], 0, 0)

    recv(nT.at[frows(partner)], nt_s.at[1], nt_r.at[1])
    add_proj(partner)
    for d in range(2, n_wt, 2):
        src = from_wt(d)
        recv(nT.at[frows(src)], nt_s.at[d], nt_r.at[d])
        pending.append(send(nT.at[frows(src)], nT.at[frows(src)], nt_s.at[d + 1], nt_r.at[d + 1], (z, partner)))
        add_proj(src)
    for d in range(2, n_wt, 2):
        src = lax.rem(partner + n_wt - d, n_wt)
        recv(nT.at[frows(src)], nt_s.at[d + 1], nt_r.at[d + 1])
        add_proj(src)

    query = (rot(proj[:t_rows, :HD], c_tab, s_tab) * query_scale).astype(BF16)
    pair = proj[:t_rows, HD:]
    kv[0, par] = jnp.where(even, rot(pair, c_tab, s_tab), pair).astype(BF16)

    kv_out = []

    def kv_send(off, which):
        device = (z + off, w) if which == 0 else (z, partner)
        return pltpu.make_async_remote_copy(
            src_ref=kv.at[0 if which == 0 else off, par], dst_ref=kv.at[off, par], send_sem=kv_s.at[off * 2 + which],
            recv_sem=kv_r.at[off * 2 + which], device_id=device, device_id_type=MESH,
        )

    pending.append(kv_send(0, 1))
    pending[-1].start()
    for off in range(1, reach + 1):

        @pl.when(z + off < n_seq)
        def _():
            kv_send(off, 0).start()

        @pl.when(z < off)
        def _():
            kv[off] = jnp.zeros((2, t_rows, HD), BF16)

    for p in range(RB):
        nblk[p] = nT[p * BLK : (p + 1) * BLK, :]
    fin[n_seq * n_wt] = jnp.zeros((chunk, BLK), BF16)
    out_grad = og[...]
    recv(kv.at[0, 1 - par], kv_s.at[1], kv_r.at[1])
    for off in range(1, reach + 1):

        @pl.when(z >= off)
        def _():
            recv(kv.at[off, par], kv_s.at[off * 2], kv_r.at[off * 2])
            kv_send(off, 1).start()

    for off in range(1, reach + 1):

        @pl.when(z >= off)
        def _():
            recv(kv.at[off, 1 - par], kv_s.at[off * 2 + 1], kv_r.at[off * 2 + 1])

    gap = lax.broadcasted_iota(jnp.int32, (t_rows, t_rows), 0) - lax.broadcasted_iota(
        jnp.int32, (t_rows, t_rows), 1
    )
    limit = jnp.minimum(pos[...], window - 1)
    exps, tanhs = [], []
    row_total = jnp.zeros((t_rows, 1), F32)
    mixed = jnp.zeros((t_rows, HD), F32)
    for off in range(reach + 1):
        t = jnp.tanh(dot(query, kv[off, 0], 1, 1) / soft_cap)
        far = gap + off * t_rows
        e = jnp.where((far >= 0) & (far <= limit), jnp.exp(soft_cap * t), 0.0)
        exps.append(e)
        tanhs.append(t)
        row_total = row_total + jnp.sum(e, axis=1, keepdims=True)
        mixed = mixed + dot(e.astype(BF16), kv[off, 1], 1, 0)
    inv_total = 1.0 / row_total
    attn_rows = (mixed * inv_total).astype(BF16)
    attn[...] = attn_rows
    delta = jnp.sum(out_grad.astype(F32) * attn_rows.astype(F32), axis=1, keepdims=True)

    def kg_send(off, which):
        device = (z - off, w if which == 0 else partner)
        return pltpu.make_async_remote_copy(
            src_ref=kvs.at[off, which], dst_ref=kvr.at[off, which], send_sem=kg_s.at[off * 2 + which],
            recv_sem=kg_r.at[off * 2 + which], device_id=device, device_id_type=MESH,
        )

    rot_grad = jnp.zeros((t_rows, HD), F32)
    own = None
    for off in range(reach, -1, -1):
        probs = exps[off] * inv_total
        pg = dot(out_grad, kv[off, 1], 1, 1)
        low = (probs * (pg - delta) * (1.0 - tanhs[off] * tanhs[off])).astype(BF16)
        rot_grad = rot_grad + dot(low, kv[off, 0], 1, 0)
        key_g = dot(low, query, 0, 0)
        val_g = dot(probs.astype(BF16), out_grad, 0, 0)
        own = jnp.where(even, key_g, val_g)
        kvs[off, 1] = jnp.where(even, val_g, key_g).astype(BF16)
        if off == 0:
            pending.append(kg_send(0, 1))
            pending[-1].start()
        else:
            kvs[off, 0] = own.astype(BF16)

            @pl.when(z >= off)
            def _():
                kg_send(off, 0).start()
                kg_send(off, 1).start()

            @pl.when(z + off >= n_seq)
            def _():
                kvr[off] = jnp.zeros((2, t_rows, HD), BF16)

    cot[...] = jnp.zeros_like(cot)
    cot[:t_rows, :HD] = (rot(rot_grad, c_tab, -s_tab) * query_scale).astype(BF16)
    recv(kvr.at[0, 1], kg_s.at[1], kg_r.at[1])
    own = own + kvr[0, 1].astype(F32)
    for off in range(1, reach + 1):

        @pl.when(z + off < n_seq)
        def _():
            recv(kvr.at[off, 0], kg_s.at[off * 2], kg_r.at[off * 2])
            recv(kvr.at[off, 1], kg_s.at[off * 2 + 1], kg_r.at[off * 2 + 1])

        own = own + kvr[off, 0].astype(F32) + kvr[off, 1].astype(F32)
    cot[:t_rows, HD:] = jnp.where(even, rot(own, c_tab, -s_tab), own).astype(BF16)

    for o in range(n_wt):
        for r in range(CAP):
            g = dot(nblk[arrp_sm[o, CAP + r, 0]], cot[...], 1, 0)
            g = jnp.where(arrp[o, r : r + 1, :] >= RB, g[:, BLK:], g[:, :BLK]).astype(BF16)
            for j in range(BLK // chunk):
                wz[r * (BLK // chunk) + j, o * chunk : (o + 1) * chunk, :] = g[j * chunk : (j + 1) * chunk]
    for d in range(1, n_seq):
        pending.append(send(wz.at[to_seq(d)], wzr.at[d], wz_s.at[d], wz_r.at[d], (to_seq(d), w)))

    order = [*range(2, n_wt, 2), 0]
    for d in order:
        o = lax.rem(partner + d, n_wt)
        gs[frows(o), :] = dot(wd[frows(o), :], cot[...], 1, 1).astype(BF16)
        pending.append(send(gs.at[frows(o)], gr.at[d + 1], g_s.at[d + 1], g_r.at[d + 1], (z, partner)))
    for d in order:
        o = to_wt(d)
        g = dot(wd[frows(o), :], cot[...], 1, 1)
        recv(gr.at[d + 1], g_s.at[d + 1], g_r.at[d + 1])
        g = g + gr[d + 1].astype(F32)
        if d == 0:
            ngT[...] = g
        else:
            gs[frows(o), :] = g.astype(BF16)
            pending.append(send(gs.at[frows(o)], gr.at[d], g_s.at[d], g_r.at[d], (z, o)))

    part = wz[z].astype(F32)
    for d in range(1, n_seq):
        recv(wzr.at[d], wz_s.at[d], wz_r.at[d])
        part = part + wzr[d].astype(F32)
    ws[...] = part.astype(BF16)

    def crows(i):
        return pl.ds(pl.multiple_of(i * chunk, 16), chunk)

    for d in range(1, n_wt):
        o = to_wt(d)
        pending.append(send(ws.at[crows(o)], fin.at[z * n_wt + w], ow_s.at[d], ow_r.at[d], (z, o)))
    fin[z * n_wt + w] = ws[crows(w), :]

    for d in range(2, n_wt, 2):
        recv(gr.at[d], g_s.at[d], g_r.at[d])
        ngT[...] += gr[d].astype(F32)
    weighted = ngT[...] * scT[...]
    rd[0] = jnp.broadcast_to(jnp.sum(weighted * gain[...], axis=0, keepdims=True), (8, TP))
    for d in range(1, n_wt):
        pending.append(send(rd.at[0], rd.at[d], rd_s.at[d], rd_r.at[d], (z, to_wt(d))))

    for d in range(1, n_wt):
        recv(fin.at[z * n_wt + from_wt(d)], ow_s.at[d], ow_r.at[d])
    for d in range(1, n_seq):
        pending.append(send(fin.at[pl.ds(z * n_wt, n_wt)], fin.at[pl.ds(z * n_wt, n_wt)], fi_s.at[d], fi_r.at[d], (to_seq(d), w)))

    tokT[:feats, :128] = jnp.broadcast_to(jnp.sum(weighted, axis=1, keepdims=True), (feats, 128))
    gb[0] = tokT[:, :128].T[:8, :].astype(BF16).astype(F32)
    for d in range(1, n_seq):
        pending.append(send(gb.at[0], gb.at[d], gb_s.at[d], gb_r.at[d], (to_seq(d), w)))

    for d in range(1, n_wt):
        recv(rd.at[d], rd_s.at[d], rd_r.at[d])
    dots = rd[0]
    for d in range(1, n_wt):
        dots = dots + rd[d]
    dots_row = dots[0:1, :] / D
    tokT[:feats, :] = inv_row * (ngT[...] * gain[...] - scT[...] * dots_row)
    tg[...] = tokT[...].T[:t_rows, :feats].astype(BF16)

    for d in range(1, n_seq):
        recv(gb.at[d], gb_s.at[d], gb_r.at[d])
    sums = gb[0]
    for d in range(1, n_seq):
        sums = sums + gb[d]
    gg[...] = sums

    for d in range(1, n_seq):
        recv(fin.at[pl.ds(from_seq(d) * n_wt, n_wt)], fi_s.at[d], fi_r.at[d])
    per = BLK // chunk
    for s in range(slots):
        for j in range(per):
            bg[s, j * chunk : (j + 1) * chunk, :] = fin[dest[s * per + j]]

    for copy in pending:
        copy.wait_send()
    for off in range(1, reach + 1):

        @pl.when(z + off < n_seq)
        def _():
            kv_send(off, 0).wait_send()

        @pl.when(z >= off)
        def _():
            kv_send(off, 1).wait_send()
            kg_send(off, 0).wait_send()
            kg_send(off, 1).wait_send()


def body(tokens_in, norm_gain, positions, blocks, slot_code, out_grad):
    t_rows, feats = tokens_in.shape
    n_wt = lax.axis_size("wt")
    n_seq = lax.axis_size("seq")
    slots = blocks.shape[1]
    count = n_wt * CAP
    reach = n_seq // 2
    chunk = CAP * BLK // n_seq
    fp = -(-feats // 128) * 128
    half = HD // 2
    frequency = 10000.0 ** (-2.0 * jnp.arange(half, dtype=F32) / HD)
    angles = positions.astype(F32)[:, None] * frequency[None, :]
    cos, sin = jnp.cos(angles), jnp.sin(angles)
    cos = jnp.concatenate([cos, cos], axis=1)
    sin = jnp.concatenate([-sin, sin], axis=1)
    codes = slot_code[0]
    live = codes >= 0
    user = jnp.where(live, codes // POS, -1)
    ids = jnp.arange(slots, dtype=jnp.int32)
    before = (user[None, :] == user[:, None]) & (ids[None, :] < ids[:, None])
    rank = jnp.sum(before.astype(jnp.int32), axis=1)
    dest = jnp.where(live, user * CAP + rank, -1)
    hit = dest[None, :] == jnp.arange(count, dtype=jnp.int32)[:, None]
    slot_of = jnp.sum(jnp.where(hit, ids[None, :], 0), axis=1)
    spot = jnp.sum(jnp.where(hit, (codes - user * POS + 1)[None, :], 0), axis=1) - 1
    spot = spot.reshape(n_wt, CAP)
    row = jnp.maximum(jnp.where(spot >= RB, spot - RB, spot), 0)
    place = jnp.concatenate([spot, row, jnp.zeros((n_wt, 8 - 2 * CAP), jnp.int32)], axis=1)
    place = jnp.broadcast_to(place[:, :, None], (n_wt, 8, 128))
    per = BLK // chunk
    piece = (rank[:, None] * per + jnp.arange(per, dtype=jnp.int32)[None, :]) * n_wt + user[:, None]
    piece = jnp.where(live[:, None], piece, n_seq * n_wt).reshape(-1)
    vmem = pl.BlockSpec(memory_space=pltpu.VMEM)
    smem = pl.BlockSpec(memory_space=pltpu.SMEM)
    dma = lambda n: pltpu.SemaphoreType.DMA((n,))
    kvn = 2 * (reach + 1)
    attn, tg, gg, bg = pl.pallas_call(
        functools.partial(kernel, n_seq, n_wt),
        out_shape=(
            jax.ShapeDtypeStruct((t_rows, HD), BF16),
            jax.ShapeDtypeStruct((t_rows, feats), BF16),
            jax.ShapeDtypeStruct((8, fp), F32),
            jax.ShapeDtypeStruct((slots, BLK, BLK), BF16),
        ),
        in_specs=[vmem] * 6 + [smem] * 2 + [vmem] * 2,
        out_specs=(vmem,) * 4,
        scratch_shapes=[
            pltpu.VMEM((TP, fp), F32),
            pltpu.VMEM((fp, TP), F32),
            pltpu.VMEM((feats, TP), F32),
            pltpu.VMEM((feats, TP), F32),
            pltpu.VMEM((n_wt, 8, TP), F32),
            pltpu.VMEM((n_wt, 8, TP), F32),
            pltpu.VMEM((D, TP), BF16),
            pltpu.VMEM((count, BLK, BLK), BF16),
            pltpu.VMEM((count + 1, BLK, BLK), BF16),
            pltpu.VMEM((n_wt, 8, 128), jnp.int32),
            pltpu.VMEM((8, 128), jnp.int32),
            pltpu.SMEM((8, 128), jnp.int32),
            pltpu.SMEM((n_wt, 8, 128), jnp.int32),
            pltpu.VMEM((D, 2 * HD), BF16),
            pltpu.VMEM((TP, 2 * HD), F32),
            pltpu.VMEM((reach + 1, 2, t_rows, HD), BF16),
            pltpu.VMEM((reach + 1, 2, t_rows, HD), BF16),
            pltpu.VMEM((reach + 1, 2, t_rows, HD), BF16),
            pltpu.VMEM((TP, 2 * HD), BF16),
            pltpu.VMEM((n_seq, n_wt * chunk, BLK), BF16),
            pltpu.VMEM((n_seq, n_wt * chunk, BLK), BF16),
            pltpu.VMEM((n_wt * chunk, BLK), BF16),
            pltpu.VMEM((n_seq * n_wt + 1, chunk, BLK), BF16),
            pltpu.VMEM((D, TP), BF16),
            pltpu.VMEM((n_wt, feats, TP), BF16),
            pltpu.VMEM((n_seq, 8, fp), F32),
            pltpu.VMEM((RB, BLK, TP), BF16),
        ]
        + [dma(n_wt)] * 8
        + [dma(kvn)] * 4
        + [dma(n_seq)] * 2
        + [dma(n_wt)] * 2
        + [dma(n_seq)] * 2
        + [dma(n_wt)] * 4
        + [dma(n_seq)] * 2
        + [dma(2)],
        compiler_params=pltpu.CompilerParams(
            collective_id=0, has_side_effects=True, vmem_limit_bytes=56 * 1024 * 1024
        ),
    )(
        tokens_in, norm_gain[:, None], positions[:, None], cos, sin, blocks[0],
        slot_of.astype(jnp.int32), piece.astype(jnp.int32), place.astype(jnp.int32), out_grad,
    )
    return attn, tg, gg[0, :feats], bg[None]


def solution(mesh):
    placed = (
        P("seq", "wt"),
        P("wt"),
        P("seq"),
        P("wt", None, None, None),
        P("wt", None),
        P("seq", "wt"),
    )
    return jax.shard_map(
        body,
        mesh=mesh,
        in_specs=placed,
        out_specs=(P("seq", "wt"), P("seq", "wt"), P("wt"), P("wt", None, None, None)),
        check_vma=False,
    )
```
